32 devices in a mesh: groups: 2 (over y), dom: 4 (over z), rep: 2 (over x), sub: 2 (over core).
Axes of the slice: x: 2, y: 2, z: 4, core: 2. Of those that a mesh axis runs over, the one named last changes fastest.
Arguments:
- adjacency: bfloat16 [2048, 4, 256], P(('groups', 'dom'), None, 'rep'), parts along dimension 0, may hold values from 0 to 1, as said below
- block_presence_mask: int32 [16, 4, 2], P(('groups', 'dom'), None, 'rep'), parts along dimension 0, may hold values from 0 to 1, as said below
- features: bfloat16 [2048, 128], P(('groups', 'dom', 'rep')), parts along dimension 0, may hold values from -20 to 20
- weight: bfloat16 [128, 256], P(None, 'sub'), may hold values from -0.5 to 0.5
- bias: float32 [256], P('sub'), may hold values from -3 to 3
- cotangent: bfloat16 [2048, 256], P(('groups', 'dom', 'rep'), 'sub'), parts along dimension 0, may hold values from -6 to 6
Outputs:
- activation: bfloat16 [2048, 256], P(('groups', 'dom', 'rep'), 'sub'), parts along dimension 0
- grad_input: bfloat16 [2048, 128], P(('groups', 'dom', 'rep')), parts along dimension 0
- grad_weight: float32 [256, 256], P('groups', 'sub'), parts along dimension 0
The draws below stay inside these ranges and needn't reach their ends.
There are 2 independent parts, one for each index of `groups`. The reference program is written for one: setup_inputs(seed, part) draws one part's arguments, and reference() takes and returns one part's arrays. A program takes and returns all parts, laid end to end along the dimension named above; an argument that names none is the same for every part. Nothing has to cross between parts.
Inputs may be any that keep to these rules, and one draw needn't show every extreme that they name: Read as a 1024 x 1024 matrix, the adjacency is symmetric. Read as a square matrix of blocks, block_presence_mask is symmetric; every diagonal block, every block beside the diagonal, and every block whose block row and block column differ by exactly 4 is 1.
All inputs are finite; a program needn't handle non-finite values.
Results may differ from the reference program's by a relative error of at most 0.0062.
Values may be sent and summed in bfloat16 or wider, within the bound.
No kernel may reach another device: no remote copies, remote signals or barrier semaphores. Data moves between devices by JAX's collectives and lax.ppermute only.
A program may use at most 64 MiB of HBM per device.

```python
import math
import jax
import jax.numpy as jnp
from jax import lax

FEAT = 128
HIDDEN_WIDTH = 256
BLOCK = 128
NODES = 1024
N_DOM = 4


def draw_adjacency(key, part):
    key = jax.random.fold_in(key, 11)
    first = jax.random.fold_in(key, 0)
    node_total = NODES
    scale = 2.0 * (6.0 * BLOCK) ** (-0.5)
    base = jax.random.uniform(first, (node_total, node_total), jnp.float32, 0.0, 1.0)
    mirror = (base + base.T) * 0.5
    return (mirror * scale).reshape(node_total, N_DOM, node_total // N_DOM).astype(jnp.bfloat16)


def draw_block_presence_mask(key, part):
    key = jax.random.fold_in(key, 23)
    first, second = jax.random.split(key)
    block_count_total = NODES // BLOCK
    levels = jax.random.randint(first, (block_count_total,), 1, 5)
    noise = jax.random.randint(second, (block_count_total, block_count_total), 0, 60)
    total = jnp.minimum(noise, noise.T)
    index = jnp.arange(block_count_total)
    offset = jnp.abs(index[:, None] - index[None, :])
    band = offset <= 1
    across = offset == block_count_total // 2
    live = (total < levels[:, None] + levels[None, :]) | band | across
    return live.astype(jnp.int32).reshape(block_count_total, N_DOM, block_count_total // N_DOM)


def draw_features(key, part):
    key = jax.random.fold_in(key, 37)
    first = jax.random.fold_in(key, 0)
    ramp = 3.0 ** (jnp.arange(NODES, dtype=jnp.float32) / NODES)
    values = jnp.clip(jax.random.normal(first, (NODES, FEAT), jnp.float32), -6.0, 6.0)
    return (values * ramp[:, None]).astype(jnp.bfloat16)


def steps_of(stream_key, extent, shards, smallest, high):
    def one(dim, parts):
        draws = jax.random.uniform(jax.random.fold_in(jax.random.fold_in(stream_key, 6), dim), (parts,), jnp.float32, smallest / len(shards), high / len(shards))
        return jnp.repeat(jnp.exp(draws), extent[dim] // parts).reshape((-1,) + (1,) * (len(extent) - dim - 1))

    factor_of = one(*shards[0])
    for cut in shards[1:]:
        factor_of = factor_of * one(*cut)
    return factor_of


def centred(own_key, shape, deviation, limit, pieces=(), kind=jnp.bfloat16):
    values = jax.random.normal(own_key, shape, jnp.float32) * deviation
    if len(pieces) > 0:
        values = steps_of(own_key, shape, pieces, -0.22, 0.18) * values
    return jnp.clip(values, min=-limit, max=limit).astype(kind)


def setup_inputs(seed: int = 0, part: int = 0) -> dict:
    splits = jax.random.split(jax.random.key(seed), 7)
    part_keys = jax.random.split(jax.random.fold_in(splits[6], part), 7)
    return {
        "adjacency": draw_adjacency(jax.random.fold_in(jax.random.fold_in(splits[6], part), 71), part),
        "block_presence_mask": draw_block_presence_mask(jax.random.fold_in(jax.random.fold_in(splits[6], part), 71), part),
        "features": draw_features(jax.random.fold_in(jax.random.fold_in(splits[6], part), 71), part),
        "weight": centred(splits[3], (FEAT, HIDDEN_WIDTH), FEAT ** -0.5, 0.5, ((1, 2),)),
        "bias": centred(splits[4], (HIDDEN_WIDTH,), 0.5, 3.0, ((0, 2),), jnp.float32),
        "cotangent": centred(part_keys[5], (NODES, HIDDEN_WIDTH), 1.0, 6.0, ((0, 8), (1, 2))),
    }


def reference(adjacency, block_presence_mask, features, weight, bias, cotangent):
    node_total = NODES
    block_extent = BLOCK
    block_count_total = node_total // block_extent
    stacked_blocks = adjacency.reshape(block_count_total, block_extent, node_total)
    block_alive_flags = block_presence_mask.reshape(block_count_total, block_count_total).astype(jnp.bfloat16)
    support = jnp.dot(features, weight, preferred_element_type=jnp.float32).astype(jnp.bfloat16)

    def forward_pass_rows(pair):
        rows, flags = pair
        effective = rows * jnp.repeat(flags, block_extent, total_repeat_length=node_total)[None, :]
        return jnp.dot(effective, support, preferred_element_type=jnp.float32)
    matmul_product = lax.map(forward_pass_rows, (stacked_blocks, block_alive_flags)).reshape(node_total, HIDDEN_WIDTH)
    pre = matmul_product + bias[None, :]
    sigma = jax.nn.sigmoid(pre)
    activation = (pre * sigma).astype(jnp.bfloat16)
    grad_pre = (cotangent.astype(jnp.float32) * sigma * (1.0 + pre * (1.0 - sigma))).astype(jnp.bfloat16)
    gradient_block_list = grad_pre.reshape(block_count_total, block_extent, HIDDEN_WIDTH)

    def reverse_pass_rows(carry, triple):
        rows, flags, grads = triple
        effective = rows * jnp.repeat(flags, block_extent, total_repeat_length=node_total)[None, :]
        term = lax.dot_general(effective, grads, (((0,), (0,)), ((), ())), preferred_element_type=jnp.float32)
        return (carry + term, None)
    start_offset = jnp.zeros((node_total, HIDDEN_WIDTH), jnp.float32)
    gradient_of_support, unused_slot = lax.scan(reverse_pass_rows, start_offset, (stacked_blocks, block_alive_flags, gradient_block_list))
    grad_weight = jnp.dot(features.astype(jnp.float32).T, gradient_of_support, precision=lax.Precision.HIGHEST) / math.sqrt(node_total)
    grad_input = jnp.dot(gradient_of_support, weight.astype(jnp.float32).T, precision=lax.Precision.HIGHEST).astype(jnp.bfloat16)
    return (activation, grad_input, grad_weight)
```

```python
import math

import jax
import jax.numpy as jnp
from jax import lax
from jax.experimental import pallas as pl
from jax.experimental.pallas import tpu as pltpu
from jax.sharding import PartitionSpec as P

CHIPS = ("dom", "rep")
CORES = ("dom", "rep", "sub")
F32 = jnp.float32
BF16 = jnp.bfloat16


def forward_and_gp(operator, features, weight, bias, cotangent):
    z = jnp.dot(operator, features, preferred_element_type=F32)
    high = z.astype(BF16)
    low = (z - high.astype(F32)).astype(BF16)
    both = jnp.concatenate([high, low], axis=1)
    pre = jnp.dot(both, jnp.concatenate([weight, weight], axis=0), preferred_element_type=F32) + bias
    sigma = jax.nn.sigmoid(pre)
    activation = (pre * sigma).astype(BF16)
    grad_pre = (cotangent.astype(F32) * sigma * (1.0 + pre * (1.0 - sigma))).astype(BF16)
    back = lax.dot_general(
        grad_pre, weight, (((1,), (1,)), ((), ())), preferred_element_type=F32
    ).astype(BF16)
    return high, low, activation, grad_pre, back


def weight_term(high, low, grads):
    return lax.dot_general(
        jnp.concatenate([high, low], axis=0),
        jnp.concatenate([grads, grads], axis=0),
        (((0,), (0,)), ((), ())),
        preferred_element_type=F32,
    )


def masked_rows(adjacency, mask, which, nodes):
    _, sections, width = adjacency.shape
    per = mask.shape[0] * nodes // adjacency.shape[0]
    rows = lax.dynamic_slice_in_dim(adjacency, which * nodes, nodes, axis=0)
    flags = lax.dynamic_slice_in_dim(mask, which * per, per, axis=0).astype(BF16)
    flags = jnp.broadcast_to(
        flags[:, None, :, :, None],
        (per, nodes // per, sections, mask.shape[2], width // mask.shape[2]),
    ).reshape(nodes, sections, width)
    return (rows * flags).transpose(1, 0, 2)


def general(mesh, adjacency, mask, features, weight, bias, cotangent):
    reps = mesh.shape["rep"]
    nodes, width = features.shape[0], adjacency.shape[2]
    sections = adjacency.shape[1]
    pieces = jnp.stack([masked_rows(adjacency, mask, q, nodes) for q in range(reps)])
    pieces = lax.all_to_all(pieces, "rep", 0, 0, tiled=True)
    operator = pieces.transpose(2, 1, 0, 3).reshape(nodes, sections * reps * width)
    everyone = lax.all_gather(features, CHIPS, axis=0, tiled=True)
    whole_weight = lax.all_gather(weight, "sub", axis=1, tiled=True)
    whole_bias = lax.all_gather(bias, "sub", axis=0, tiled=True)
    whole_cotangent = lax.all_gather(cotangent, "sub", axis=1, tiled=True)
    high, low, activation, grad_pre, back = forward_and_gp(
        operator, everyone, whole_weight, whole_bias[None, :], whole_cotangent
    )
    half = weight.shape[1]
    mine = lax.axis_index("sub") * half
    activation = lax.dynamic_slice_in_dim(activation, mine, half, axis=1)
    grads = lax.dynamic_slice_in_dim(grad_pre, mine, half, axis=1)
    total = lax.psum(weight_term(high, low, grads), CHIPS)
    backs = lax.all_gather(back, CHIPS, axis=0, tiled=True)
    grad_input = jnp.dot(operator, backs, preferred_element_type=F32).astype(BF16)
    return activation, grad_input, total / math.sqrt(sections * reps * width)


SHARED = (((3, 1), (2, 1)), ((2, 0), (3, 0)), ((1, 0), (1, 1)))


def fetch(value, first, second=None):
    pairs = []
    for d in range(4):
        for r in range(2):
            for c, off in enumerate((first, first if second is None else second)):
                source = (d * 2 + r) * 2 + c
                pairs.append((source, ((d ^ off[0]) * 2 + (r ^ off[1])) * 2 + c))
    return lax.ppermute(value, CORES, pairs)


def swap(value):
    return lax.ppermute(value, "sub", [(0, 1), (1, 0)])


def vmem_call(body, outs, *operands):
    return pl.pallas_call(
        body,
        out_shape=outs,
        in_specs=[pl.BlockSpec(memory_space=pltpu.VMEM)] * len(operands),
        out_specs=[pl.BlockSpec(memory_space=pltpu.VMEM)] * len(outs),
    )(*operands)


def in_order(first, second):
    zero = lax.axis_index("sub") == 0
    return jnp.where(zero, first, second), jnp.where(zero, second, first)


def operator_rows(own, other, offsets):
    d = lax.axis_index("dom")
    return jnp.concatenate([(other if rx else own)[d ^ dx] for dx, rx in offsets], axis=1)


def ordered_offsets(pairs):
    return [off for pair in pairs for off in pair]


def forward_kernel(own, other, x, x0, x1, x2, y0, y1, y2, w, w_, b, b_, g, g_, act, msg):
    n = x.shape[0]
    blocks = [x[...], other[4]]
    for direct, swapped in ((x0, y0), (x1, y1), (x2, y2)):
        blocks += in_order(direct[...], swapped[...])
    rows = operator_rows(own, other, [(0, 0), (0, 1)] + ordered_offsets(SHARED))
    weight = jnp.concatenate(in_order(w[...], w_[...]), axis=1)
    bias = jnp.concatenate(in_order(b[...], b_[...]), axis=1)
    cotangent = jnp.concatenate(in_order(g[...], g_[...]), axis=1)
    high, low, activation, grad_pre, back = forward_and_gp(
        rows, jnp.concatenate(blocks, axis=0), weight, bias, cotangent
    )
    half = w.shape[1]
    zero = lax.axis_index("sub") == 0
    act[...] = jnp.where(zero, activation[:, :half], activation[:, half:])
    grads = jnp.where(zero, grad_pre[:, :half], grad_pre[:, half:])
    term = weight_term(high, low, grads)
    msg[:n] = back
    upper = term.astype(BF16)
    msg[n : 2 * n] = upper
    msg[2 * n :] = (term - upper.astype(F32)).astype(BF16)


NEAR = ((0, 1), (1, 0), (1, 1))
FAR = SHARED[:2]


def plane_sum_kernel(n, a, b, c, d, out):
    def term(ref):
        return ref[n : 2 * n].astype(F32) + ref[2 * n :].astype(F32)

    out[...] = (term(a) + term(b)) + (term(c) + term(d))


def backward_kernel(own, other, m, m0, m1, m2, v0, v1, u0, u1, gi):
    n = own.shape[1]
    blocks = [m[:n], m0[:n], m1[:n], m2[:n]]
    for direct, swapped in ((v0, u0), (v1, u1)):
        blocks += in_order(direct[...], swapped[...])
    rows = operator_rows(own, other, [(0, 0)] + list(NEAR) + ordered_offsets(FAR))
    gi[...] = jnp.dot(rows, jnp.concatenate(blocks, axis=0), preferred_element_type=F32).astype(BF16)


def direct(mesh, adjacency, mask, features, weight, bias, cotangent):
    nodes, feat = features.shape
    sections, width = adjacency.shape[1:]
    half = weight.shape[1]
    r = lax.axis_index("rep")

    xs = [fetch(features, *pair) for pair in SHARED]
    give = masked_rows(adjacency, mask, 1 - r, nodes)
    other = fetch(jnp.concatenate([give, features[None]], axis=0), (0, 1))
    own = masked_rows(adjacency, mask, r, nodes)
    row = bias[None, :]
    w_, b_, g_ = swap(weight), swap(row), swap(cotangent)
    ys = [swap(x) for x in xs]
    act, msg = vmem_call(
        forward_kernel,
        [
            jax.ShapeDtypeStruct((nodes, half), BF16),
            jax.ShapeDtypeStruct((nodes + 2 * feat, half), BF16),
        ],
        own, other, features, *xs, *ys, weight, w_, row, b_, cotangent, g_,
    )
    near = [fetch(msg, off) for off in NEAR]
    back = msg[:nodes]
    far = [fetch(back, *pair) for pair in FAR]
    (plane,) = vmem_call(
        lambda *refs: plane_sum_kernel(nodes, *refs),
        [jax.ShapeDtypeStruct((feat, half), F32)],
        msg, *near,
    )
    across = fetch(plane, (2, 0))
    swapped = [swap(v) for v in far]
    (grad_input,) = vmem_call(
        backward_kernel,
        [jax.ShapeDtypeStruct((nodes, feat), BF16)],
        own, other, msg, *near, *far, *swapped,
    )
    total = (plane + across) / math.sqrt(sections * 2 * width)
    return act, grad_input, total


def solution(mesh):
    small = dict(mesh.shape) == {"groups": mesh.shape["groups"], "dom": 4, "rep": 2, "sub": 2}
    body = direct if small else general
    return jax.shard_map(
        lambda *arrays: body(mesh, *arrays),
        mesh=mesh,
        in_specs=(
            P(("groups", "dom"), None, "rep"),
            P(("groups", "dom"), None, "rep"),
            P(("groups", "dom", "rep"), None),
            P(None, "sub"),
            P("sub"),
            P(("groups", "dom", "rep"), "sub"),
        ),
        out_specs=(
            P(("groups", "dom", "rep"), "sub"),
            P(("groups", "dom", "rep"), None),
            P("groups", "sub"),
        ),
        check_vma=False,
    )
```

```python
import math

import jax
import jax.numpy as jnp
from jax import lax
from jax.experimental import pallas as pl
from jax.experimental.pallas import tpu as pltpu
from jax.sharding import PartitionSpec as P

CHIPS = ("dom", "rep")
CORES = ("dom", "rep", "sub")
F32 = jnp.float32
BF16 = jnp.bfloat16


def forward_and_gp(operator, features, weight, bias, cotangent):
    z = jnp.dot(operator, features, preferred_element_type=F32)
    high = z.astype(BF16)
    low = (z - high.astype(F32)).astype(BF16)
    both = jnp.concatenate([high, low], axis=1)
    pre = jnp.dot(both, jnp.concatenate([weight, weight], axis=0), preferred_element_type=F32) + bias
    sigma = jax.nn.sigmoid(pre)
    activation = (pre * sigma).astype(BF16)
    grad_pre = (cotangent.astype(F32) * sigma * (1.0 + pre * (1.0 - sigma))).astype(BF16)
    back = lax.dot_general(
        grad_pre, weight, (((1,), (1,)), ((), ())), preferred_element_type=F32
    ).astype(BF16)
    return high, low, activation, grad_pre, back


def weight_term(high, low, grads):
    return lax.dot_general(
        jnp.concatenate([high, low], axis=0),
        jnp.concatenate([grads, grads], axis=0),
        (((0,), (0,)), ((), ())),
        preferred_element_type=F32,
    )


def masked_rows(adjacency, mask, start, count):
    _, sections, width = adjacency.shape
    extent = adjacency.shape[0] // mask.shape[0]
    rows = lax.dynamic_slice_in_dim(adjacency, start, count, axis=0)
    tall = max(1, count // extent)
    flags = lax.dynamic_slice_in_dim(mask, start // extent, tall, axis=0).astype(BF16)
    flags = jnp.broadcast_to(
        flags[:, None, :, :, None],
        (tall, count // tall, sections, mask.shape[2], width // mask.shape[2]),
    ).reshape(count, sections, width)
    return (rows * flags).transpose(1, 0, 2)


def general(mesh, adjacency, mask, features, weight, bias, cotangent):
    reps = mesh.shape["rep"]
    nodes, width = features.shape[0], adjacency.shape[2]
    sections = adjacency.shape[1]
    pieces = jnp.stack([masked_rows(adjacency, mask, q * nodes, nodes) for q in range(reps)])
    pieces = lax.all_to_all(pieces, "rep", 0, 0, tiled=True)
    operator = pieces.transpose(2, 1, 0, 3).reshape(nodes, sections * reps * width)
    everyone = lax.all_gather(features, CHIPS, axis=0, tiled=True)
    whole_weight = lax.all_gather(weight, "sub", axis=1, tiled=True)
    whole_bias = lax.all_gather(bias, "sub", axis=0, tiled=True)
    whole_cotangent = lax.all_gather(cotangent, "sub", axis=1, tiled=True)
    high, low, activation, grad_pre, back = forward_and_gp(
        operator, everyone, whole_weight, whole_bias[None, :], whole_cotangent
    )
    half = weight.shape[1]
    mine = lax.axis_index("sub") * half
    activation = lax.dynamic_slice_in_dim(activation, mine, half, axis=1)
    grads = lax.dynamic_slice_in_dim(grad_pre, mine, half, axis=1)
    total = lax.psum(weight_term(high, low, grads), CHIPS)
    backs = lax.all_gather(back, CHIPS, axis=0, tiled=True)
    grad_input = jnp.dot(operator, backs, preferred_element_type=F32).astype(BF16)
    return activation, grad_input, total / math.sqrt(sections * reps * width)


SHARED = (((3, 1), (2, 1)), ((2, 0), (3, 0)), ((1, 0), (1, 1)))
ACROSS = ((3, 0), (2, 0), (1, 0))


def fetch(value, first, second=None):
    pairs = []
    for d in range(4):
        for r in range(2):
            for c, off in enumerate((first, first if second is None else second)):
                source = (d * 2 + r) * 2 + c
                pairs.append((source, ((d ^ off[0]) * 2 + (r ^ off[1])) * 2 + c))
    return lax.ppermute(value, CORES, pairs)


def swap(value):
    return lax.ppermute(value, "sub", [(0, 1), (1, 0)])


def vmem(*shape, dtype=BF16):
    return pltpu.VMEM(shape, dtype)


def vmem_call(body, outs, *operands):
    held = [pltpu.with_memory_space_constraint(x, pltpu.VMEM) for x in operands]
    return pl.pallas_call(
        body,
        out_shape=outs,
        in_specs=[pl.BlockSpec(memory_space=pltpu.VMEM)] * len(operands),
        out_specs=[pl.BlockSpec(memory_space=pltpu.VMEM)] * len(outs),
    )(*held)


def load_kernel(count, *refs):
    sources, targets, sems = refs[:count], refs[count : 2 * count], refs[-1]
    copies = [
        pltpu.make_async_copy(source, target, sems.at[i])
        for i, (source, target) in enumerate(zip(sources, targets))
    ]
    for copy in copies:
        copy.start()
    for copy in copies:
        copy.wait()


def load(*arrays):
    return pl.pallas_call(
        lambda *refs: load_kernel(len(arrays), *refs),
        out_shape=[pltpu.VMEM(x.shape, x.dtype) for x in arrays],
        in_specs=[pl.BlockSpec(memory_space=pl.ANY)] * len(arrays),
        out_specs=[pl.BlockSpec(memory_space=pltpu.VMEM)] * len(arrays),
        scratch_shapes=[pltpu.SemaphoreType.DMA((len(arrays),))],
    )(*arrays)


def in_order(first, second):
    zero = lax.axis_index("sub") == 0
    return jnp.where(zero, first, second), jnp.where(zero, second, first)


def forward_kernel(own, p, q, x, x0, x1, x2, y0, y1, y2, w, w_, b, b_, g, g_, act, back, msg, mine, rows, xs):
    n = x.shape[0]
    sections = own.shape[0]
    d, r, c = (lax.axis_index(a) for a in CORES)

    def columns(s, rep):
        return pl.ds(pl.multiple_of((s * 2 + rep) * n, n), n)

    first, second = in_order(p[...], q[...])
    for s in range(sections):
        rows[:, columns(s, r)] = own[s]
        rows[:n, columns(s, 1 - r)] = first[s * n : (s + 1) * n]
        rows[n:, columns(s, 1 - r)] = second[s * n : (s + 1) * n]
    low, high = (sections + 1) * n, (sections + 1) * n + n // 2
    xs[columns(d, r), :] = x[...]
    xs[columns(d, 1 - r), :] = jnp.concatenate([first[low:high], second[low:high]], axis=0)
    for pair, direct, swapped in zip(SHARED, (x0, x1, x2), (y0, y1, y2)):
        for (dx, rx), value in zip(pair, in_order(direct[...], swapped[...])):
            xs[columns(d ^ dx, r ^ rx), :] = value
    mine[...] = rows[pl.ds(pl.multiple_of(r * n, n), n), :]

    weight = jnp.concatenate(in_order(w[...], w_[...]), axis=1)
    bias = jnp.concatenate(in_order(b[...], b_[...]), axis=1)
    here = jnp.concatenate(in_order(g[...], g_[...]), axis=1)
    there = jnp.concatenate([first[sections * n : low], second[sections * n : low]], axis=1)
    zero = r == 0
    cotangent = jnp.concatenate(
        [jnp.where(zero, here, there), jnp.where(zero, there, here)], axis=0
    )
    high, low, activation, grad_pre, v = forward_and_gp(
        rows[...], xs[...], weight, bias, cotangent
    )
    half = w.shape[1]
    zero = c == 0
    activation = jnp.where(r == 0, activation[:n], activation[n:])
    act[...] = jnp.where(zero, activation[:, :half], activation[:, half:])
    grads = jnp.where(zero, grad_pre[:, :half], grad_pre[:, half:])
    back[...] = v
    msg[:n] = jnp.where(zero, v[:n], v[n:])
    msg[n:] = weight_term(high, low, grads).astype(BF16)


def backward_kernel(scale, rows, back, msg, m0, m1, m2, s0, s1, s2, a, gi, gw, act, vs):
    n = rows.shape[0]
    d = lax.axis_index("dom")
    act[...] = a[...]
    terms = {(0, 0): msg[n:].astype(F32)}
    vs[pl.ds(pl.multiple_of(d * 2 * n, n), 2 * n), :] = back[...]
    for off, direct, swapped in zip(ACROSS, (m0, m1, m2), (s0, s1, s2)):
        terms[off] = direct[n:].astype(F32)
        both = jnp.concatenate(in_order(direct[:n], swapped[:n]), axis=0)
        vs[pl.ds(pl.multiple_of((d ^ off[0]) * 2 * n, n), 2 * n), :] = both
    gw[...] = ((terms[0, 0] + terms[1, 0]) + (terms[2, 0] + terms[3, 0])) * scale
    gi[...] = jnp.dot(rows[...], vs[...], preferred_element_type=F32).astype(BF16)


def direct(mesh, adjacency, mask, features, weight, bias, cotangent):
    nodes, feat = features.shape
    sections, width = adjacency.shape[1:]
    total = sections * 2 * width
    half = weight.shape[1]
    c = lax.axis_index("sub")
    few = nodes // 2

    far = fetch(features, *SHARED[0])
    adj, held, grads, flags = load(adjacency, features, cotangent, mask.transpose(0, 2, 1))
    operator = masked_rows(adj, flags.transpose(0, 2, 1), 0, 2 * nodes)
    give = lax.dynamic_slice_in_dim(operator, c * nodes, nodes, axis=1).reshape(sections * nodes, width)
    give = jnp.concatenate([give, grads, lax.dynamic_slice_in_dim(held, c * few, few)], axis=0)
    taken = fetch(give, (0, 1))
    xs = [far] + [fetch(features, *pair) for pair in SHARED[1:]]
    row = bias[None, :]
    w_, b_, g_ = swap(weight), swap(row), swap(cotangent)
    ys = [swap(x) for x in xs]
    act, back, msg, mine = pl.pallas_call(
        forward_kernel,
        out_shape=[vmem(nodes, half), vmem(2 * nodes, feat), vmem(nodes + feat, half), vmem(nodes, total)],
        in_specs=[pl.BlockSpec(memory_space=pltpu.VMEM)] * 16,
        out_specs=[pl.BlockSpec(memory_space=pltpu.VMEM)] * 4,
        scratch_shapes=[vmem(2 * nodes, total), vmem(total, feat)],
    )(
        *(
            pltpu.with_memory_space_constraint(x, pltpu.VMEM)
            for x in (operator, taken, swap(taken), held, *xs, *ys, weight, w_, row, b_, grads, g_)
        )
    )
    ms = [fetch(msg, off) for off in ACROSS]
    ss = [swap(m) for m in ms]
    scale = 1.0 / math.sqrt(total)
    grad_input, grad_weight, activation = pl.pallas_call(
        lambda *refs: backward_kernel(scale, *refs),
        out_shape=[
            jax.ShapeDtypeStruct((nodes, feat), BF16),
            jax.ShapeDtypeStruct((feat, half), F32),
            jax.ShapeDtypeStruct((nodes, half), BF16),
        ],
        in_specs=[pl.BlockSpec(memory_space=pltpu.VMEM)] * 10,
        out_specs=[pl.BlockSpec(memory_space=pltpu.VMEM)] * 3,
        scratch_shapes=[vmem(total, feat)],
    )(
        *(
            pltpu.with_memory_space_constraint(x, pltpu.VMEM)
            for x in (mine, back, msg, *ms, *ss, act)
        )
    )
    return activation, grad_input, grad_weight


def solution(mesh):
    small = dict(mesh.shape) == {"groups": mesh.shape["groups"], "dom": 4, "rep": 2, "sub": 2}
    body = direct if small else general
    return jax.shard_map(
        lambda *arrays: body(mesh, *arrays),
        mesh=mesh,
        in_specs=(
            P(("groups", "dom"), None, "rep"),
            P(("groups", "dom"), None, "rep"),
            P(("groups", "dom", "rep"), None),
            P(None, "sub"),
            P("sub"),
            P(("groups", "dom", "rep"), "sub"),
        ),
        out_specs=(
            P(("groups", "dom", "rep"), "sub"),
            P(("groups", "dom", "rep"), None),
            P("groups", "sub"),
        ),
        check_vma=False,
    )
```

```python
import math

import jax
import jax.numpy as jnp
from jax import lax
from jax.experimental import pallas as pl
from jax.experimental.pallas import tpu as pltpu
from jax.sharding import PartitionSpec as P

CHIPS = ("dom", "rep")
CORES = ("dom", "rep", "sub")
F32 = jnp.float32
BF16 = jnp.bfloat16


def forward_and_gp(operator, features, weight, bias, cotangent):
    z = jnp.dot(operator, features, preferred_element_type=F32)
    high = z.astype(BF16)
    low = (z - high.astype(F32)).astype(BF16)
    both = jnp.concatenate([high, low], axis=1)
    pre = jnp.dot(both, jnp.concatenate([weight, weight], axis=0), preferred_element_type=F32) + bias
    sigma = jax.nn.sigmoid(pre)
    activation = (pre * sigma).astype(BF16)
    grad_pre = (cotangent.astype(F32) * sigma * (1.0 + pre * (1.0 - sigma))).astype(BF16)
    back = lax.dot_general(
        grad_pre, weight, (((1,), (1,)), ((), ())), preferred_element_type=F32
    ).astype(BF16)
    return high, low, activation, grad_pre, back


def weight_term(high, low, grads):
    return lax.dot_general(
        jnp.concatenate([high, low], axis=0),
        jnp.concatenate([grads, grads], axis=0),
        (((0,), (0,)), ((), ())),
        preferred_element_type=F32,
    )


def masked_rows(adjacency, mask, start, count):
    _, sections, width = adjacency.shape
    extent = adjacency.shape[0] // mask.shape[0]
    rows = lax.dynamic_slice_in_dim(adjacency, start, count, axis=0)
    tall = max(1, count // extent)
    flags = lax.dynamic_slice_in_dim(mask, start // extent, tall, axis=0).astype(BF16)
    flags = jnp.broadcast_to(
        flags[:, None, :, :, None],
        (tall, count // tall, sections, mask.shape[2], width // mask.shape[2]),
    ).reshape(count, sections, width)
    return (rows * flags).transpose(1, 0, 2)


def general(mesh, adjacency, mask, features, weight, bias, cotangent):
    reps = mesh.shape["rep"]
    nodes, width = features.shape[0], adjacency.shape[2]
    sections = adjacency.shape[1]
    pieces = jnp.stack([masked_rows(adjacency, mask, q * nodes, nodes) for q in range(reps)])
    pieces = lax.all_to_all(pieces, "rep", 0, 0, tiled=True)
    operator = pieces.transpose(2, 1, 0, 3).reshape(nodes, sections * reps * width)
    everyone = lax.all_gather(features, CHIPS, axis=0, tiled=True)
    whole_weight = lax.all_gather(weight, "sub", axis=1, tiled=True)
    whole_bias = lax.all_gather(bias, "sub", axis=0, tiled=True)
    whole_cotangent = lax.all_gather(cotangent, "sub", axis=1, tiled=True)
    high, low, activation, grad_pre, back = forward_and_gp(
        operator, everyone, whole_weight, whole_bias[None, :], whole_cotangent
    )
    half = weight.shape[1]
    mine = lax.axis_index("sub") * half
    activation = lax.dynamic_slice_in_dim(activation, mine, half, axis=1)
    grads = lax.dynamic_slice_in_dim(grad_pre, mine, half, axis=1)
    total = lax.psum(weight_term(high, low, grads), CHIPS)
    backs = lax.all_gather(back, CHIPS, axis=0, tiled=True)
    grad_input = jnp.dot(operator, backs, preferred_element_type=F32).astype(BF16)
    return activation, grad_input, total / math.sqrt(sections * reps * width)


SHARED = (((3, 1), (3, 0)), ((1, 0), (1, 1)), ((2, 0), (2, 1)))
ACROSS = ((3, 0), (1, 0), (2, 0))


def fetch(value, first, second=None):
    pairs = []
    for d in range(4):
        for r in range(2):
            for c, off in enumerate((first, first if second is None else second)):
                source = (d * 2 + r) * 2 + c
                pairs.append((source, ((d ^ off[0]) * 2 + (r ^ off[1])) * 2 + c))
    return lax.ppermute(value, CORES, pairs)


def swap(value):
    return lax.ppermute(value, "sub", [(0, 1), (1, 0)])


def vmem(*shape, dtype=BF16):
    return pltpu.VMEM(shape, dtype)


def vmem_call(body, outs, *operands):
    held = [pltpu.with_memory_space_constraint(x, pltpu.VMEM) for x in operands]
    return pl.pallas_call(
        body,
        out_shape=outs,
        in_specs=[pl.BlockSpec(memory_space=pltpu.VMEM)] * len(operands),
        out_specs=[pl.BlockSpec(memory_space=pltpu.VMEM)] * len(outs),
    )(*held)


def load_kernel(a, x, g, w, m, b, ao, xo, go, wo, mo, parts, held, sems):
    pairs = ((a, ao), (x, xo), (g, go), (w, wo), (m, mo), (b, held))
    copies = [pltpu.make_async_copy(p, q, sems.at[i]) for i, (p, q) in enumerate(pairs)]
    for copy in copies:
        copy.start()
    for copy in copies[::-1]:
        copy.wait()
        if copy is copies[-1]:
            rest = held[...]
            for i in range(3):
                part = rest.astype(BF16)
                parts[i : i + 1] = part
                rest = rest - part.astype(F32)


def load(*arrays):
    row = arrays[-1]
    outs = [pltpu.VMEM(x.shape, x.dtype) for x in arrays[:-1]] + [vmem(16, row.shape[1])]
    return pl.pallas_call(
        load_kernel,
        out_shape=outs,
        in_specs=[pl.BlockSpec(memory_space=pl.ANY)] * len(arrays),
        out_specs=[pl.BlockSpec(memory_space=pltpu.VMEM)] * len(outs),
        scratch_shapes=[
            pltpu.VMEM(row.shape, row.dtype),
            pltpu.SemaphoreType.DMA((len(arrays),)),
        ],
    )(*arrays)


def in_order(first, second):
    zero = lax.axis_index("sub") == 0
    return jnp.where(zero, first, second), jnp.where(zero, second, first)


def mask_rows(entries, blocks, sections):
    row = lax.broadcasted_iota(jnp.int32, entries.shape, 0)
    lane = lax.broadcasted_iota(jnp.int32, entries.shape, 1)
    picked = jnp.zeros(entries.shape, F32)
    for q in range(blocks):
        here = (row // sections == q) & (lane == row % sections)
        picked = jnp.where(here, entries[q : q + 1].astype(F32), picked)
    ones = jnp.ones((entries.shape[1],) * 2, BF16)
    return jnp.dot(picked.astype(BF16), ones, preferred_element_type=F32).astype(BF16)


def pack_kernel(*refs):
    at = 0
    for ref in refs[:-1]:
        refs[-1][at : at + ref.shape[0]] = ref[...]
        at += ref.shape[0]


def forward_kernel(own, give, x, here, there, act, back, msg, mine, rows, xs):
    n = x.shape[0]
    sections = own.shape[0]
    d, r, c = (lax.axis_index(a) for a in CORES)

    def columns(s, rep):
        return pl.ds(pl.multiple_of((s * 2 + rep) * n, n), n)

    low, high = (sections + 1) * n, (sections + 1) * n + n // 2
    end = give.shape[0]
    flags = mask_rows(give[high:end], 2, sections)
    flags_ = mask_rows(here[high:end], 2, sections)
    first, second = in_order(here[...], there[...])
    for s in range(sections):
        for k, part in enumerate((first, second)):
            at = slice(k * n, (k + 1) * n)
            entry = slice(k * sections + s, k * sections + s + 1)
            rows[at, columns(s, r)] = own[s, at] * flags[entry]
            rows[at, columns(s, 1 - r)] = part[s * n : (s + 1) * n] * flags_[entry]
    xs[columns(d, r), :] = x[...]
    xs[columns(d, 1 - r), :] = jnp.concatenate([first[low:high], second[low:high]], axis=0)
    for i, pair in enumerate(SHARED):
        for (dx, rx), part in zip(pair, (first, second)):
            xs[columns(d ^ dx, r ^ rx), :] = part[end + i * n : end + (i + 1) * n]
    end += len(SHARED) * n
    mine[...] = rows[pl.ds(pl.multiple_of(r * n, n), n), :]

    weight, ours = (
        jnp.concatenate([part[k : k + n] for part in (first, second)], axis=1)
        for k in (end, end + n)
    )
    end += 2 * n
    bias = jnp.concatenate(
        [jnp.sum(part[end : end + 3].astype(F32), axis=0, keepdims=True) for part in (first, second)],
        axis=1,
    )
    theirs = jnp.concatenate([part[sections * n : low] for part in (first, second)], axis=1)
    zero = r == 0
    cotangent = jnp.concatenate(
        [jnp.where(zero, ours, theirs), jnp.where(zero, theirs, ours)], axis=0
    )
    high, low, activation, grad_pre, v = forward_and_gp(
        rows[...], xs[...], weight, bias, cotangent
    )
    half = msg.shape[1]
    zero = c == 0
    activation = jnp.where(r == 0, activation[:n], activation[n:])
    act[...] = jnp.where(zero, activation[:, :half], activation[:, half:])
    grads = jnp.where(zero, grad_pre[:, :half], grad_pre[:, half:])
    back[...] = v
    msg[:n] = jnp.where(zero, v[:n], v[n:])
    msg[n:] = weight_term(high, low, grads).astype(BF16)


def backward_kernel(scale, rows, back, msg, m0, m1, m2, s0, s1, s2, a, gi, gw, act, vs):
    n = rows.shape[0]
    d = lax.axis_index("dom")
    act[...] = a[...]
    terms = {(0, 0): msg[n:].astype(F32)}
    vs[pl.ds(pl.multiple_of(d * 2 * n, n), 2 * n), :] = back[...]
    for off, direct, swapped in zip(ACROSS, (m0, m1, m2), (s0, s1, s2)):
        terms[off] = direct[n:].astype(F32)
        both = jnp.concatenate(in_order(direct[:n], swapped[:n]), axis=0)
        vs[pl.ds(pl.multiple_of((d ^ off[0]) * 2 * n, n), 2 * n), :] = both
    gw[...] = ((terms[0, 0] + terms[1, 0]) + (terms[2, 0] + terms[3, 0])) * scale
    gi[...] = jnp.dot(rows[...], vs[...], preferred_element_type=F32).astype(BF16)


def direct(mesh, adjacency, mask, features, weight, bias, cotangent):
    nodes, feat = features.shape
    sections, width = adjacency.shape[1:]
    total = sections * 2 * width
    half = weight.shape[1]
    c = lax.axis_index("sub")
    few = nodes // 2


    adj, held, grads, wide, flat, row = load(
        adjacency, features, cotangent, weight, mask.transpose(0, 2, 1), bias[None, :]
    )
    own = adj.transpose(1, 0, 2)
    give = lax.dynamic_slice_in_dim(adj, c * nodes, nodes, axis=0).transpose(1, 0, 2)
    flat = jnp.pad(flat[:, 0].astype(BF16), ((0, 14), (0, width - sections)))
    give = jnp.concatenate(
        [give.reshape(sections * nodes, width), grads, lax.dynamic_slice_in_dim(held, c * few, few), flat],
        axis=0,
    )
    taken = fetch(give, (0, 1))
    xs = [fetch(features, *pair) for pair in SHARED]
    parts = (taken, *xs, wide, grads, row)
    (here,) = vmem_call(pack_kernel, [vmem(sum(x.shape[0] for x in parts), width)], *parts)
    there = swap(here)
    act, back, msg, mine = pl.pallas_call(
        forward_kernel,
        out_shape=[vmem(nodes, half), vmem(2 * nodes, feat), vmem(nodes + feat, half), vmem(nodes, total)],
        in_specs=[pl.BlockSpec(memory_space=pltpu.VMEM)] * 5,
        out_specs=[pl.BlockSpec(memory_space=pltpu.VMEM)] * 4,
        scratch_shapes=[vmem(2 * nodes, total), vmem(total, feat)],
    )(
        *(
            pltpu.with_memory_space_constraint(x, pltpu.VMEM)
            for x in (own, give, held, here, there)
        )
    )
    ms = [fetch(msg, off) for off in ACROSS]
    ss = [swap(m) for m in ms]
    scale = 1.0 / math.sqrt(total)
    grad_input, grad_weight, activation = pl.pallas_call(
        lambda *refs: backward_kernel(scale, *refs),
        out_shape=[
            jax.ShapeDtypeStruct((nodes, feat), BF16),
            jax.ShapeDtypeStruct((feat, half), F32),
            jax.ShapeDtypeStruct((nodes, half), BF16),
        ],
        in_specs=[pl.BlockSpec(memory_space=pltpu.VMEM)] * 10,
        out_specs=[pl.BlockSpec(memory_space=pltpu.VMEM)] * 3,
        scratch_shapes=[vmem(total, feat)],
    )(
        *(
            pltpu.with_memory_space_constraint(x, pltpu.VMEM)
            for x in (mine, back, msg, *ms, *ss, act)
        )
    )
    return activation, grad_input, grad_weight


def solution(mesh):
    small = dict(mesh.shape) == {"groups": mesh.shape["groups"], "dom": 4, "rep": 2, "sub": 2}
    body = direct if small else general
    return jax.shard_map(
        lambda *arrays: body(mesh, *arrays),
        mesh=mesh,
        in_specs=(
            P(("groups", "dom"), None, "rep"),
            P(("groups", "dom"), None, "rep"),
            P(("groups", "dom", "rep"), None),
            P(None, "sub"),
            P("sub"),
            P(("groups", "dom", "rep"), "sub"),
        ),
        out_specs=(
            P(("groups", "dom", "rep"), "sub"),
            P(("groups", "dom", "rep"), None),
            P("groups", "sub"),
        ),
        check_vma=False,
    )
```

```python
import math

import jax
import jax.numpy as jnp
from jax import lax
from jax.experimental import pallas as pl
from jax.experimental.pallas import tpu as pltpu
from jax.sharding import PartitionSpec as P

CHIPS = ("dom", "rep")
CORES = ("dom", "rep", "sub")
F32 = jnp.float32
BF16 = jnp.bfloat16


def forward_and_gp(operator, features, weight, bias, cotangent):
    z = jnp.dot(operator, features, preferred_element_type=F32)
    high = z.astype(BF16)
    low = (z - high.astype(F32)).astype(BF16)
    both = jnp.concatenate([high, low], axis=1)
    pre = jnp.dot(both, jnp.concatenate([weight, weight], axis=0), preferred_element_type=F32) + bias
    sigma = jax.nn.sigmoid(pre)
    activation = (pre * sigma).astype(BF16)
    grad_pre = (cotangent.astype(F32) * sigma * (1.0 + pre * (1.0 - sigma))).astype(BF16)
    back = lax.dot_general(
        grad_pre, weight, (((1,), (1,)), ((), ())), preferred_element_type=F32
    )
    return high, low, activation, grad_pre, back


def transposed_dot(a, b):
    return lax.dot_general(a, b, (((0,), (0,)), ((), ())), preferred_element_type=F32)


def weight_term(high, low, grads):
    return transposed_dot(
        jnp.concatenate([high, low], axis=0), jnp.concatenate([grads, grads], axis=0)
    )


def masked_rows(adjacency, mask, start, count):
    _, sections, width = adjacency.shape
    extent = adjacency.shape[0] // mask.shape[0]
    rows = lax.dynamic_slice_in_dim(adjacency, start, count, axis=0)
    tall = max(1, count // extent)
    flags = lax.dynamic_slice_in_dim(mask, start // extent, tall, axis=0).astype(BF16)
    flags = jnp.broadcast_to(
        flags[:, None, :, :, None],
        (tall, count // tall, sections, mask.shape[2], width // mask.shape[2]),
    ).reshape(count, sections, width)
    return (rows * flags).transpose(1, 0, 2)


def general(mesh, adjacency, mask, features, weight, bias, cotangent):
    reps = mesh.shape["rep"]
    nodes, width = features.shape[0], adjacency.shape[2]
    sections = adjacency.shape[1]
    pieces = jnp.stack([masked_rows(adjacency, mask, q * nodes, nodes) for q in range(reps)])
    pieces = lax.all_to_all(pieces, "rep", 0, 0, tiled=True)
    operator = pieces.transpose(2, 1, 0, 3).reshape(nodes, sections * reps * width)
    everyone = lax.all_gather(features, CHIPS, axis=0, tiled=True)
    whole_weight = lax.all_gather(weight, "sub", axis=1, tiled=True)
    whole_bias = lax.all_gather(bias, "sub", axis=0, tiled=True)
    whole_cotangent = lax.all_gather(cotangent, "sub", axis=1, tiled=True)
    high, low, activation, grad_pre, back = forward_and_gp(
        operator, everyone, whole_weight, whole_bias[None, :], whole_cotangent
    )
    half = weight.shape[1]
    mine = lax.axis_index("sub") * half
    activation = lax.dynamic_slice_in_dim(activation, mine, half, axis=1)
    grads = lax.dynamic_slice_in_dim(grad_pre, mine, half, axis=1)
    total = lax.psum(weight_term(high, low, grads), CHIPS)
    backs = lax.all_gather(back.astype(BF16), CHIPS, axis=0, tiled=True)
    grad_input = jnp.dot(operator, backs, preferred_element_type=F32).astype(BF16)
    return activation, grad_input, total / math.sqrt(sections * reps * width)


SHARED = (((3, 1), (3, 0)), ((1, 0), (1, 1)), ((2, 0), (2, 1)))
ACROSS = ((3, 0), (2, 0))


def fetch(value, first, second=None):
    pairs = []
    for d in range(4):
        for r in range(2):
            for c, off in enumerate((first, first if second is None else second)):
                source = (d * 2 + r) * 2 + c
                pairs.append((source, ((d ^ off[0]) * 2 + (r ^ off[1])) * 2 + c))
    return lax.ppermute(value, CORES, pairs)


def swap(value):
    return lax.ppermute(value, "sub", [(0, 1), (1, 0)])


def vmem(*shape, dtype=BF16):
    return pltpu.VMEM(shape, dtype)


def vmem_call(body, outs, *operands):
    held = [pltpu.with_memory_space_constraint(x, pltpu.VMEM) for x in operands]
    return pl.pallas_call(
        body,
        out_shape=outs,
        in_specs=[pl.BlockSpec(memory_space=pltpu.VMEM)] * len(operands),
        out_specs=[pl.BlockSpec(memory_space=pltpu.VMEM)] * len(outs),
    )(*held)


def load_kernel(a, x, g, m, ao, fo, go, mo, sems):
    c = lax.axis_index("sub")
    pairs = (
        (a.at[pl.ds(c * ao.shape[0], ao.shape[0])], ao),
        (x.at[pl.ds(pl.multiple_of(c * fo.shape[0], 16), fo.shape[0])], fo),
        (g, go),
        (m, mo),
    )
    copies = [pltpu.make_async_copy(p, q, sems.at[i]) for i, (p, q) in enumerate(pairs)]
    for copy in copies:
        copy.start()
    for copy in copies:
        copy.wait()


def load(adjacency, features, cotangent, mask):
    arrays = (adjacency, features, cotangent, mask)
    outs = [vmem(x.shape[0] // 2, *x.shape[1:]) for x in arrays[:2]]
    outs += [pltpu.VMEM(x.shape, x.dtype) for x in arrays[2:]]
    return pl.pallas_call(
        load_kernel,
        out_shape=outs,
        in_specs=[pl.BlockSpec(memory_space=pl.ANY)] * len(arrays),
        out_specs=[pl.BlockSpec(memory_space=pltpu.VMEM)] * len(outs),
        scratch_shapes=[pltpu.SemaphoreType.DMA((len(outs),))],
    )(*arrays)


def in_order(first, second):
    zero = lax.axis_index("sub") == 0
    return jnp.where(zero, first, second), jnp.where(zero, second, first)


def mask_rows(entries, blocks, sections):
    row = lax.broadcasted_iota(jnp.int32, entries.shape, 0)
    lane = lax.broadcasted_iota(jnp.int32, entries.shape, 1)
    picked = jnp.zeros(entries.shape, F32)
    for q in range(blocks):
        here = (row // sections == q) & (lane == row % sections)
        picked = jnp.where(here, entries[q : q + 1].astype(F32), picked)
    ones = jnp.ones((entries.shape[1],) * 2, BF16)
    return jnp.dot(picked.astype(BF16), ones, preferred_element_type=F32).astype(BF16)


def pack_kernel(*refs):
    *arrays, row, out = refs
    at = 0
    for ref in arrays:
        out[at : at + ref.shape[0]] = ref[...]
        at += ref.shape[0]
    rest = row[...]
    for i in range(3):
        part = rest.astype(BF16)
        out[at + i : at + i + 1] = part
        rest = rest - part.astype(F32)


def forward_kernel(own, give, x, here, there, act, far, near, kept, rows, xs):
    n = x.shape[0]
    sections = own.shape[0]
    d, r, c = (lax.axis_index(a) for a in CORES)

    def columns(s, rep):
        return pl.ds(pl.multiple_of((s * 2 + rep) * n, n), n)

    low, high = (sections + 1) * n, (sections + 1) * n + n // 2
    end = give.shape[0]
    flags = mask_rows(give[high:end], 2, sections)
    flags_ = mask_rows(here[high:end], 2, sections)
    first, second = in_order(here[...], there[...])
    for s in range(sections):
        for k, part in enumerate((first, second)):
            at = slice(k * n, (k + 1) * n)
            entry = slice(k * sections + s, k * sections + s + 1)
            rows[at, columns(s, r)] = own[s, at] * flags[entry]
            rows[at, columns(s, 1 - r)] = part[s * n : (s + 1) * n] * flags_[entry]
    xs[columns(d, r), :] = x[...]
    xs[columns(d, 1 - r), :] = jnp.concatenate([first[low:high], second[low:high]], axis=0)
    for i, pair in enumerate(SHARED):
        for (dx, rx), part in zip(pair, (first, second)):
            xs[columns(d ^ dx, r ^ rx), :] = part[end + i * n : end + (i + 1) * n]
    end += len(SHARED) * n

    weight, ours = (
        jnp.concatenate([part[k : k + n] for part in (first, second)], axis=1)
        for k in (end, end + n)
    )
    end += 2 * n
    bias = jnp.concatenate(
        [jnp.sum(part[end : end + 3].astype(F32), axis=0, keepdims=True) for part in (first, second)],
        axis=1,
    )
    theirs = jnp.concatenate([part[sections * n : low] for part in (first, second)], axis=1)
    zero = r == 0
    cotangent = jnp.concatenate(
        [jnp.where(zero, ours, theirs), jnp.where(zero, theirs, ours)], axis=0
    )
    high, low, activation, grad_pre, v = forward_and_gp(
        rows[...], xs[...], weight, bias, cotangent
    )
    half = far.shape[1]
    zero = c == 0
    activation = jnp.where(r == 0, activation[:n], activation[n:])
    act[...] = jnp.where(zero, activation[:, :half], activation[:, half:])
    term = weight_term(high, low, grad_pre).astype(BF16)
    far[n : 2 * n] = term[:, :half]
    far[2 * n :] = term[:, half:]
    near[n // 2 :] = jnp.where(zero, term[:, :half], term[:, half:])

    upper = v.astype(BF16)
    lower = (v - upper.astype(F32)).astype(BF16)
    v = jnp.concatenate([upper, lower], axis=0)

    def give_back(s):
        block = rows[:, columns(s, r)]
        return transposed_dot(jnp.concatenate([block, block], axis=0), v)

    kept[...] = give_back(d)
    aside = give_back(d ^ 1).astype(BF16)
    near[: n // 2] = jnp.where(zero, aside[: n // 2], aside[n // 2 :])
    far[:n] = give_back(d ^ jnp.where(zero, ACROSS[0][0], ACROSS[1][0])).astype(BF16)


def far_term(ref, core, n):
    return ref[pl.ds(pl.multiple_of((1 + core) * n, n), n), :]


def pack_back_kernel(far, near, out):
    n = far.shape[0] // 3
    out[:n] = far[:n]
    out[n : 2 * n] = far_term(far, 1 - lax.axis_index("sub"), n)
    out[2 * n :] = near[: n // 2]


def backward_kernel(scale, kept, mine, far, near, there, a, gi, gw, act):
    n = kept.shape[0]
    c = lax.axis_index("sub")
    act[...] = a[...]
    parts = {0: kept[...], 1: jnp.concatenate(in_order(near[: n // 2], there[2 * n :]), axis=0)}
    terms = {0: far_term(mine, c, n), 1: near[n // 2 :]}
    for (dx, _), part, term in zip(
        ACROSS, in_order(far[:n], there[:n]), in_order(far_term(far, c, n), there[n : 2 * n])
    ):
        parts[dx], terms[dx] = part, term

    def total(values):
        values = [values[dx].astype(F32) for dx in range(4)]
        return (values[0] + values[1]) + (values[2] + values[3])

    gw[...] = total(terms) * scale
    gi[...] = total(parts).astype(BF16)


def direct(mesh, adjacency, mask, features, weight, bias, cotangent):
    nodes, feat = features.shape
    sections, width = adjacency.shape[1:]
    total = sections * 2 * width
    half = weight.shape[1]
    c = lax.axis_index("sub")


    x0 = fetch(features, *SHARED[0])
    x2 = fetch(features, *SHARED[2])
    give, few, grads, flat = load(adjacency, features, cotangent, mask.transpose(0, 2, 1))
    own = adjacency.transpose(1, 0, 2)
    give = give.transpose(1, 0, 2)
    flat = jnp.pad(flat[:, 0].astype(BF16), ((0, 14), (0, width - sections)))
    give = jnp.concatenate(
        [give.reshape(sections * nodes, width), grads, few, flat],
        axis=0,
    )
    late, give = lax.optimization_barrier((features, give))
    x1 = fetch(late, *SHARED[1])
    taken = fetch(give, (0, 1))
    xs = [x0, x1, x2]
    parts = (taken, *xs, weight, grads, bias[None, :])
    (here,) = vmem_call(pack_kernel, [vmem(sum(x.shape[0] for x in parts) + 15, width)], *parts)
    there = swap(here)
    act, far, near, kept = pl.pallas_call(
        forward_kernel,
        out_shape=[
            vmem(nodes, half),
            vmem(3 * nodes, feat),
            vmem(nodes + nodes // 2, feat),
            vmem(nodes, feat, dtype=F32),
        ],
        in_specs=[pl.BlockSpec(memory_space=pltpu.VMEM)] * 5,
        out_specs=[pl.BlockSpec(memory_space=pltpu.VMEM)] * 4,
        scratch_shapes=[vmem(2 * nodes, total), vmem(total, feat)],
    )(
        *(
            pltpu.with_memory_space_constraint(x, pltpu.VMEM)
            for x in (own, give, features, here, there)
        )
    )
    far_, near_ = fetch(far, *ACROSS), fetch(near, (1, 0))
    (packed,) = vmem_call(pack_back_kernel, [vmem(2 * nodes + nodes // 2, feat)], far_, near_)
    packed = swap(packed)
    scale = 1.0 / math.sqrt(total)
    grad_input, grad_weight, activation = pl.pallas_call(
        lambda *refs: backward_kernel(scale, *refs),
        out_shape=[
            jax.ShapeDtypeStruct((nodes, feat), BF16),
            jax.ShapeDtypeStruct((feat, half), F32),
            jax.ShapeDtypeStruct((nodes, half), BF16),
        ],
        in_specs=[pl.BlockSpec(memory_space=pltpu.VMEM)] * 6,
        out_specs=[pl.BlockSpec(memory_space=pltpu.VMEM)] * 3,
    )(
        *(
            pltpu.with_memory_space_constraint(x, pltpu.VMEM)
            for x in (kept, far, far_, near_, packed, act)
        )
    )
    return activation, grad_input, grad_weight


def solution(mesh):
    small = dict(mesh.shape) == {"groups": mesh.shape["groups"], "dom": 4, "rep": 2, "sub": 2}
    body = direct if small else general
    return jax.shard_map(
        lambda *arrays: body(mesh, *arrays),
        mesh=mesh,
        in_specs=(
            P(("groups", "dom"), None, "rep"),
            P(("groups", "dom"), None, "rep"),
            P(("groups", "dom", "rep"), None),
            P(None, "sub"),
            P("sub"),
            P(("groups", "dom", "rep"), "sub"),
        ),
        out_specs=(
            P(("groups", "dom", "rep"), "sub"),
            P(("groups", "dom", "rep"), None),
            P("groups", "sub"),
        ),
        check_vma=False,
    )
```

```python
import math

import jax
import jax.numpy as jnp
from jax import lax
from jax.experimental import pallas as pl
from jax.experimental.pallas import tpu as pltpu
from jax.sharding import PartitionSpec as P

CHIPS = ("dom", "rep")
CORES = ("dom", "rep", "sub")
F32 = jnp.float32
BF16 = jnp.bfloat16


def forward_and_gp(operator, features, weight, bias, cotangent):
    z = jnp.dot(operator, features, preferred_element_type=F32)
    high = z.astype(BF16)
    low = (z - high.astype(F32)).astype(BF16)
    both = jnp.concatenate([high, low], axis=1)
    pre = jnp.dot(both, jnp.concatenate([weight, weight], axis=0), preferred_element_type=F32) + bias
    sigma = jax.nn.sigmoid(pre)
    activation = (pre * sigma).astype(BF16)
    grad_pre = (cotangent.astype(F32) * sigma * (1.0 + pre * (1.0 - sigma))).astype(BF16)
    back = lax.dot_general(
        grad_pre, weight, (((1,), (1,)), ((), ())), preferred_element_type=F32
    )
    return high, low, activation, grad_pre, back


def transposed_dot(a, b):
    return lax.dot_general(a, b, (((0,), (0,)), ((), ())), preferred_element_type=F32)


def weight_term(high, low, grads):
    return transposed_dot(
        jnp.concatenate([high, low], axis=0), jnp.concatenate([grads, grads], axis=0)
    )


def masked_rows(adjacency, mask, start, count):
    _, sections, width = adjacency.shape
    extent = adjacency.shape[0] // mask.shape[0]
    rows = lax.dynamic_slice_in_dim(adjacency, start, count, axis=0)
    tall = max(1, count // extent)
    flags = lax.dynamic_slice_in_dim(mask, start // extent, tall, axis=0).astype(BF16)
    flags = jnp.broadcast_to(
        flags[:, None, :, :, None],
        (tall, count // tall, sections, mask.shape[2], width // mask.shape[2]),
    ).reshape(count, sections, width)
    return (rows * flags).transpose(1, 0, 2)


def general(mesh, adjacency, mask, features, weight, bias, cotangent):
    reps = mesh.shape["rep"]
    nodes, width = features.shape[0], adjacency.shape[2]
    sections = adjacency.shape[1]
    pieces = jnp.stack([masked_rows(adjacency, mask, q * nodes, nodes) for q in range(reps)])
    pieces = lax.all_to_all(pieces, "rep", 0, 0, tiled=True)
    operator = pieces.transpose(2, 1, 0, 3).reshape(nodes, sections * reps * width)
    everyone = lax.all_gather(features, CHIPS, axis=0, tiled=True)
    whole_weight = lax.all_gather(weight, "sub", axis=1, tiled=True)
    whole_bias = lax.all_gather(bias, "sub", axis=0, tiled=True)
    whole_cotangent = lax.all_gather(cotangent, "sub", axis=1, tiled=True)
    high, low, activation, grad_pre, back = forward_and_gp(
        operator, everyone, whole_weight, whole_bias[None, :], whole_cotangent
    )
    half = weight.shape[1]
    mine = lax.axis_index("sub") * half
    activation = lax.dynamic_slice_in_dim(activation, mine, half, axis=1)
    grads = lax.dynamic_slice_in_dim(grad_pre, mine, half, axis=1)
    total = lax.psum(weight_term(high, low, grads), CHIPS)
    backs = lax.all_gather(back.astype(BF16), CHIPS, axis=0, tiled=True)
    grad_input = jnp.dot(operator, backs, preferred_element_type=F32).astype(BF16)
    return activation, grad_input, total / math.sqrt(sections * reps * width)


SHARED = (((3, 1), (3, 0)), ((1, 0), (1, 1)), ((2, 0), (2, 1)))
ACROSS = ((3, 0), (2, 0))


def fetch(value, first, second=None):
    pairs = []
    for d in range(4):
        for r in range(2):
            for c, off in enumerate((first, first if second is None else second)):
                source = (d * 2 + r) * 2 + c
                pairs.append((source, ((d ^ off[0]) * 2 + (r ^ off[1])) * 2 + c))
    return lax.ppermute(value, CORES, pairs)


def swap(value):
    return lax.ppermute(value, "sub", [(0, 1), (1, 0)])


def vmem(*shape, dtype=BF16):
    return pltpu.VMEM(shape, dtype)


def vmem_call(body, outs, *operands):
    held = [pltpu.with_memory_space_constraint(x, pltpu.VMEM) for x in operands]
    return pl.pallas_call(
        body,
        out_shape=outs,
        in_specs=[pl.BlockSpec(memory_space=pltpu.VMEM)] * len(operands),
        out_specs=[pl.BlockSpec(memory_space=pltpu.VMEM)] * len(outs),
    )(*held)


def load_kernel(a, x, g, m, ao, fo, go, mo, sems):
    c = lax.axis_index("sub")
    pairs = (
        (a.at[pl.ds(c * ao.shape[0], ao.shape[0])], ao),
        (x.at[pl.ds(pl.multiple_of(c * fo.shape[0], 16), fo.shape[0])], fo),
        (g, go),
        (m, mo),
    )
    copies = [pltpu.make_async_copy(p, q, sems.at[i]) for i, (p, q) in enumerate(pairs)]
    for copy in copies:
        copy.start()
    for copy in copies:
        copy.wait()


def load(adjacency, features, cotangent, mask):
    arrays = (adjacency, features, cotangent, mask)
    outs = [vmem(x.shape[0] // 2, *x.shape[1:]) for x in arrays[:2]]
    outs += [pltpu.VMEM(x.shape, x.dtype) for x in arrays[2:]]
    return pl.pallas_call(
        load_kernel,
        out_shape=outs,
        in_specs=[pl.BlockSpec(memory_space=pl.ANY)] * len(arrays),
        out_specs=[pl.BlockSpec(memory_space=pltpu.VMEM)] * len(outs),
        scratch_shapes=[pltpu.SemaphoreType.DMA((len(outs),))],
    )(*arrays)


def in_order(first, second):
    zero = lax.axis_index("sub") == 0
    return jnp.where(zero, first, second), jnp.where(zero, second, first)


def mask_rows(entries, blocks, sections):
    row = lax.broadcasted_iota(jnp.int32, entries.shape, 0)
    lane = lax.broadcasted_iota(jnp.int32, entries.shape, 1)
    picked = jnp.zeros(entries.shape, F32)
    for q in range(blocks):
        here = (row // sections == q) & (lane == row % sections)
        picked = jnp.where(here, entries[q : q + 1].astype(F32), picked)
    ones = jnp.ones((entries.shape[1],) * 2, BF16)
    return jnp.dot(picked.astype(BF16), ones, preferred_element_type=F32).astype(BF16)


def pack_kernel(*refs):
    *arrays, row, out = refs
    at = 0
    for ref in arrays:
        out[at : at + ref.shape[0]] = ref[...]
        at += ref.shape[0]
    rest = row[...]
    tail = jnp.zeros((out.shape[0] - at, rest.shape[1]), F32)
    line = lax.broadcasted_iota(jnp.int32, tail.shape, 0)
    for i in range(3):
        part = rest.astype(BF16).astype(F32)
        tail = jnp.where(line == i, part, tail)
        rest = rest - part
    out[at:] = tail.astype(BF16)


def forward_kernel(own, give, x, p, q, here, there, act, far, near, kept, rows, xs):
    n = x.shape[0]
    sections = own.shape[0]
    d, r, c = (lax.axis_index(a) for a in CORES)

    def columns(s, rep):
        return pl.ds(pl.multiple_of((s * 2 + rep) * n, n), n)

    low, high = (sections + 1) * n, (sections + 1) * n + n // 2
    end = give.shape[0]
    flags = mask_rows(give[high:end], 2, sections)
    flags_ = mask_rows(p[high:end], 2, sections)
    first, second = in_order(p[:end], q[:end])
    for s in range(sections):
        for k, part in enumerate((first, second)):
            at = slice(k * n, (k + 1) * n)
            entry = slice(k * sections + s, k * sections + s + 1)
            rows[at, columns(s, r)] = own[s, at] * flags[entry]
            rows[at, columns(s, 1 - r)] = part[s * n : (s + 1) * n] * flags_[entry]
    xs[columns(d, r), :] = x[...]
    xs[columns(d, 1 - r), :] = jnp.concatenate([first[low:high], second[low:high]], axis=0)
    sides = in_order(here[...], there[...])
    for i, pair in enumerate(SHARED):
        for (dx, rx), part in zip(pair, sides):
            xs[columns(d ^ dx, r ^ rx), :] = part[i * n : (i + 1) * n]
    end = len(SHARED) * n

    weight, ours = (
        jnp.concatenate([part[k : k + n] for part in sides], axis=1)
        for k in (end, end + n)
    )
    end += 2 * n
    bias = jnp.concatenate(
        [jnp.sum(part[end : end + 3].astype(F32), axis=0, keepdims=True) for part in sides],
        axis=1,
    )
    theirs = jnp.concatenate([part[sections * n : low] for part in (first, second)], axis=1)
    zero = r == 0
    cotangent = jnp.concatenate(
        [jnp.where(zero, ours, theirs), jnp.where(zero, theirs, ours)], axis=0
    )
    high, low, activation, grad_pre, v = forward_and_gp(
        rows[...], xs[...], weight, bias, cotangent
    )
    half = far.shape[1]
    zero = c == 0
    activation = jnp.where(r == 0, activation[:n], activation[n:])
    act[...] = jnp.where(zero, activation[:, :half], activation[:, half:])
    term = weight_term(high, low, grad_pre).astype(BF16)
    far[n : 2 * n] = term[:, :half]
    far[2 * n :] = term[:, half:]
    near[n // 2 :] = jnp.where(zero, term[:, :half], term[:, half:])

    upper = v.astype(BF16)
    lower = (v - upper.astype(F32)).astype(BF16)
    v = jnp.concatenate([upper, lower], axis=0)

    def give_back(s):
        block = rows[:, columns(s, r)]
        return transposed_dot(jnp.concatenate([block, block], axis=0), v)

    kept[...] = give_back(d)
    aside = give_back(d ^ 1).astype(BF16)
    near[: n // 2] = jnp.where(zero, aside[: n // 2], aside[n // 2 :])
    far[:n] = give_back(d ^ jnp.where(zero, ACROSS[0][0], ACROSS[1][0])).astype(BF16)


def far_term(ref, core, n):
    return ref[pl.ds(pl.multiple_of((1 + core) * n, n), n), :]


def pack_back_kernel(far, near, out):
    n = far.shape[0] // 3
    out[:n] = far[:n]
    out[n : 2 * n] = far_term(far, 1 - lax.axis_index("sub"), n)
    out[2 * n :] = near[: n // 2]


def backward_kernel(scale, kept, mine, far, near, there, a, gi, gw, act):
    n = kept.shape[0]
    c = lax.axis_index("sub")
    act[...] = a[...]
    parts = {0: kept[...], 1: jnp.concatenate(in_order(near[: n // 2], there[2 * n :]), axis=0)}
    terms = {0: far_term(mine, c, n), 1: near[n // 2 :]}
    for (dx, _), part, term in zip(
        ACROSS, in_order(far[:n], there[:n]), in_order(far_term(far, c, n), there[n : 2 * n])
    ):
        parts[dx], terms[dx] = part, term

    def total(values):
        values = [values[dx].astype(F32) for dx in range(4)]
        return (values[0] + values[1]) + (values[2] + values[3])

    gw[...] = total(terms) * scale
    gi[...] = total(parts).astype(BF16)


def direct(mesh, adjacency, mask, features, weight, bias, cotangent):
    nodes, feat = features.shape
    sections, width = adjacency.shape[1:]
    total = sections * 2 * width
    half = weight.shape[1]
    x0 = fetch(features, *SHARED[0])
    x2 = fetch(features, *SHARED[2])
    give, few, grads, flat = load(adjacency, features, cotangent, mask.transpose(0, 2, 1))
    own = adjacency.transpose(1, 0, 2)
    give = give.transpose(1, 0, 2)
    flat = jnp.pad(flat[:, 0].astype(BF16), ((0, 14), (0, width - sections)))
    give = jnp.concatenate(
        [give.reshape(sections * nodes, width), grads, few, flat],
        axis=0,
    )
    late, give = lax.optimization_barrier((features, give))
    x1 = fetch(late, *SHARED[1])
    taken = fetch(give, (0, 1))
    xs = [x0, x1, x2]
    q = swap(taken)
    parts = (*xs, weight, grads, bias[None, :])
    (here,) = vmem_call(pack_kernel, [vmem(sum(x.shape[0] for x in parts) + 15, width)], *parts)
    there = swap(here)
    act, far, near, kept = pl.pallas_call(
        forward_kernel,
        out_shape=[
            vmem(nodes, half),
            vmem(3 * nodes, feat),
            vmem(nodes + nodes // 2, feat),
            vmem(nodes, feat, dtype=F32),
        ],
        in_specs=[pl.BlockSpec(memory_space=pltpu.VMEM)] * 7,
        out_specs=[pl.BlockSpec(memory_space=pltpu.VMEM)] * 4,
        scratch_shapes=[vmem(2 * nodes, total), vmem(total, feat)],
    )(
        *(
            pltpu.with_memory_space_constraint(x, pltpu.VMEM)
            for x in (own, give, features, taken, q, here, there)
        )
    )
    far_, near_ = fetch(far, *ACROSS), fetch(near, (1, 0))
    (packed,) = vmem_call(pack_back_kernel, [vmem(2 * nodes + nodes // 2, feat)], far_, near_)
    packed = swap(packed)
    scale = 1.0 / math.sqrt(total)
    grad_input, grad_weight, activation = pl.pallas_call(
        lambda *refs: backward_kernel(scale, *refs),
        out_shape=[
            jax.ShapeDtypeStruct((nodes, feat), BF16),
            jax.ShapeDtypeStruct((feat, half), F32),
            jax.ShapeDtypeStruct((nodes, half), BF16),
        ],
        in_specs=[pl.BlockSpec(memory_space=pltpu.VMEM)] * 6,
        out_specs=[pl.BlockSpec(memory_space=pltpu.VMEM)] * 3,
    )(
        *(
            pltpu.with_memory_space_constraint(x, pltpu.VMEM)
            for x in (kept, far, far_, near_, packed, act)
        )
    )
    return activation, grad_input, grad_weight


def solution(mesh):
    small = dict(mesh.shape) == {"groups": mesh.shape["groups"], "dom": 4, "rep": 2, "sub": 2}
    body = direct if small else general
    return jax.shard_map(
        lambda *arrays: body(mesh, *arrays),
        mesh=mesh,
        in_specs=(
            P(("groups", "dom"), None, "rep"),
            P(("groups", "dom"), None, "rep"),
            P(("groups", "dom", "rep"), None),
            P(None, "sub"),
            P("sub"),
            P(("groups", "dom", "rep"), "sub"),
        ),
        out_specs=(
            P(("groups", "dom", "rep"), "sub"),
            P(("groups", "dom", "rep"), None),
            P("groups", "sub"),
        ),
        check_vma=False,
    )
```

```python
import math

import jax
import jax.numpy as jnp
from jax import lax
from jax.experimental import pallas as pl
from jax.experimental.pallas import tpu as pltpu
from jax.sharding import PartitionSpec as P

CHIPS = ("dom", "rep")
CORES = ("dom", "rep", "sub")
F32 = jnp.float32
BF16 = jnp.bfloat16


def forward_and_gp(operator, features, weight, bias, cotangent):
    z = jnp.dot(operator, features, preferred_element_type=F32)
    high = z.astype(BF16)
    low = (z - high.astype(F32)).astype(BF16)
    both = jnp.concatenate([high, low], axis=1)
    pre = jnp.dot(both, jnp.concatenate([weight, weight], axis=0), preferred_element_type=F32) + bias
    sigma = jax.nn.sigmoid(pre)
    activation = (pre * sigma).astype(BF16)
    grad_pre = (cotangent.astype(F32) * sigma * (1.0 + pre * (1.0 - sigma))).astype(BF16)
    back = lax.dot_general(
        grad_pre, weight, (((1,), (1,)), ((), ())), preferred_element_type=F32
    )
    return high, low, activation, grad_pre, back


def transposed_dot(a, b):
    return lax.dot_general(a, b, (((0,), (0,)), ((), ())), preferred_element_type=F32)


def weight_term(high, low, grads):
    return transposed_dot(
        jnp.concatenate([high, low], axis=0), jnp.concatenate([grads, grads], axis=0)
    )


def masked_rows(adjacency, mask, start, count):
    _, sections, width = adjacency.shape
    extent = adjacency.shape[0] // mask.shape[0]
    rows = lax.dynamic_slice_in_dim(adjacency, start, count, axis=0)
    tall = max(1, count // extent)
    flags = lax.dynamic_slice_in_dim(mask, start // extent, tall, axis=0).astype(BF16)
    flags = jnp.broadcast_to(
        flags[:, None, :, :, None],
        (tall, count // tall, sections, mask.shape[2], width // mask.shape[2]),
    ).reshape(count, sections, width)
    return (rows * flags).transpose(1, 0, 2)


def general(mesh, adjacency, mask, features, weight, bias, cotangent):
    reps = mesh.shape["rep"]
    nodes, width = features.shape[0], adjacency.shape[2]
    sections = adjacency.shape[1]
    pieces = jnp.stack([masked_rows(adjacency, mask, q * nodes, nodes) for q in range(reps)])
    pieces = lax.all_to_all(pieces, "rep", 0, 0, tiled=True)
    operator = pieces.transpose(2, 1, 0, 3).reshape(nodes, sections * reps * width)
    everyone = lax.all_gather(features, CHIPS, axis=0, tiled=True)
    whole_weight = lax.all_gather(weight, "sub", axis=1, tiled=True)
    whole_bias = lax.all_gather(bias, "sub", axis=0, tiled=True)
    whole_cotangent = lax.all_gather(cotangent, "sub", axis=1, tiled=True)
    high, low, activation, grad_pre, back = forward_and_gp(
        operator, everyone, whole_weight, whole_bias[None, :], whole_cotangent
    )
    half = weight.shape[1]
    mine = lax.axis_index("sub") * half
    activation = lax.dynamic_slice_in_dim(activation, mine, half, axis=1)
    grads = lax.dynamic_slice_in_dim(grad_pre, mine, half, axis=1)
    total = lax.psum(weight_term(high, low, grads), CHIPS)
    backs = lax.all_gather(back.astype(BF16), CHIPS, axis=0, tiled=True)
    grad_input = jnp.dot(operator, backs, preferred_element_type=F32).astype(BF16)
    return activation, grad_input, total / math.sqrt(sections * reps * width)


SHARED = (((3, 1), (3, 0)), ((2, 0), (2, 1)), ((1, 0), (1, 1)))
ACROSS = ((3, 0), (2, 0))


def fetch(value, first, second=None):
    pairs = []
    for d in range(4):
        for r in range(2):
            for c, off in enumerate((first, first if second is None else second)):
                source = (d * 2 + r) * 2 + c
                pairs.append((source, ((d ^ off[0]) * 2 + (r ^ off[1])) * 2 + c))
    return lax.ppermute(value, CORES, pairs)


def swap(value):
    return lax.ppermute(value, "sub", [(0, 1), (1, 0)])


def vmem(*shape, dtype=BF16):
    return pltpu.VMEM(shape, dtype)


def vmem_call(body, outs, *operands):
    held = [pltpu.with_memory_space_constraint(x, pltpu.VMEM) for x in operands]
    return pl.pallas_call(
        body,
        out_shape=outs,
        in_specs=[pl.BlockSpec(memory_space=pltpu.VMEM)] * len(operands),
        out_specs=[pl.BlockSpec(memory_space=pltpu.VMEM)] * len(outs),
    )(*held)


def load_kernel(a, x, g, m, ao, fo, go, mo, sems):
    c = lax.axis_index("sub")
    pairs = (
        (a.at[pl.ds(c * ao.shape[0], ao.shape[0])], ao),
        (x.at[pl.ds(pl.multiple_of(c * fo.shape[0], 16), fo.shape[0])], fo),
        (g, go),
        (m, mo),
    )
    copies = [pltpu.make_async_copy(p, q, sems.at[i]) for i, (p, q) in enumerate(pairs)]
    for copy in copies:
        copy.start()
    for copy in copies:
        copy.wait()


def load(adjacency, features, cotangent, mask):
    arrays = (adjacency, features, cotangent, mask)
    outs = [vmem(x.shape[0] // 2, *x.shape[1:]) for x in arrays[:2]]
    outs += [pltpu.VMEM(x.shape, x.dtype) for x in arrays[2:]]
    return pl.pallas_call(
        load_kernel,
        out_shape=outs,
        in_specs=[pl.BlockSpec(memory_space=pl.ANY)] * len(arrays),
        out_specs=[pl.BlockSpec(memory_space=pltpu.VMEM)] * len(outs),
        scratch_shapes=[pltpu.SemaphoreType.DMA((len(outs),))],
    )(*arrays)


def in_order(first, second):
    zero = lax.axis_index("sub") == 0
    return jnp.where(zero, first, second), jnp.where(zero, second, first)


def mask_rows(entries, blocks, sections):
    row = lax.broadcasted_iota(jnp.int32, entries.shape, 0)
    lane = lax.broadcasted_iota(jnp.int32, entries.shape, 1)
    picked = jnp.zeros(entries.shape, F32)
    for q in range(blocks):
        here = (row // sections == q) & (lane == row % sections)
        picked = jnp.where(here, entries[q : q + 1].astype(F32), picked)
    ones = jnp.ones((entries.shape[1],) * 2, BF16)
    return jnp.dot(picked.astype(BF16), ones, preferred_element_type=F32).astype(BF16)


def pack_kernel(*refs):
    *arrays, row, out = refs
    at = 0
    for ref in arrays:
        out[at : at + ref.shape[0]] = ref[...]
        at += ref.shape[0]
    rest = row[...]
    tail = jnp.zeros((out.shape[0] - at, rest.shape[1]), F32)
    line = lax.broadcasted_iota(jnp.int32, tail.shape, 0)
    for i in range(3):
        part = rest.astype(BF16).astype(F32)
        tail = jnp.where(line == i, part, tail)
        rest = rest - part
    out[at:] = tail.astype(BF16)


def block_columns(s, rep, n):
    return pl.ds(pl.multiple_of((s * 2 + rep) * n, n), n)


def rows_kernel(own, give, p, q, rows):
    sections = own.shape[0]
    n = own.shape[1] // 2
    r = lax.axis_index("rep")
    start, end = (sections + 1) * n + n // 2, give.shape[0]
    flags = mask_rows(give[start:end], 2, sections)
    flags_ = mask_rows(p[start:end], 2, sections)
    for k, part in enumerate(in_order(p[: sections * n], q[: sections * n])):
        at = slice(k * n, (k + 1) * n)
        for s in range(sections):
            entry = slice(k * sections + s, k * sections + s + 1)
            rows[at, block_columns(s, r, n)] = own[s, at] * flags[entry]
            rows[at, block_columns(s, 1 - r, n)] = part[s * n : (s + 1) * n] * flags_[entry]


def forward_kernel(rows, x, p, q, here, there, act, far, near, kept, xs):
    n = x.shape[0]
    sections = xs.shape[0] // (2 * n)
    d, r, c = (lax.axis_index(a) for a in CORES)

    def columns(s, rep):
        return block_columns(s, rep, n)

    high = (sections + 1) * n + n // 2
    first, second = in_order(p[sections * n : high], q[sections * n : high])
    xs[columns(d, r), :] = x[...]
    xs[columns(d, 1 - r), :] = jnp.concatenate([first[n:], second[n:]], axis=0)
    sides = in_order(here[...], there[...])
    for i, pair in enumerate(SHARED):
        for (dx, rx), part in zip(pair, sides):
            xs[columns(d ^ dx, r ^ rx), :] = part[i * n : (i + 1) * n]
    end = len(SHARED) * n

    weight, ours = (
        jnp.concatenate([part[k : k + n] for part in sides], axis=1)
        for k in (end, end + n)
    )
    end += 2 * n
    bias = jnp.concatenate(
        [jnp.sum(part[end : end + 3].astype(F32), axis=0, keepdims=True) for part in sides],
        axis=1,
    )
    theirs = jnp.concatenate([first[:n], second[:n]], axis=1)
    zero = r == 0
    cotangent = jnp.concatenate(
        [jnp.where(zero, ours, theirs), jnp.where(zero, theirs, ours)], axis=0
    )
    high, low, activation, grad_pre, v = forward_and_gp(
        rows[...], xs[...], weight, bias, cotangent
    )
    half = far.shape[1]
    zero = c == 0
    activation = jnp.where(r == 0, activation[:n], activation[n:])
    act[...] = jnp.where(zero, activation[:, :half], activation[:, half:])
    term = weight_term(high, low, grad_pre).astype(BF16)
    far[n : 2 * n] = term[:, :half]
    far[2 * n :] = term[:, half:]
    near[n // 2 :] = jnp.where(zero, term[:, :half], term[:, half:])

    upper = v.astype(BF16)
    lower = (v - upper.astype(F32)).astype(BF16)
    v = jnp.concatenate([upper, lower], axis=0)

    def give_back(s):
        block = rows[:, columns(s, r)]
        return transposed_dot(jnp.concatenate([block, block], axis=0), v)

    kept[...] = give_back(d)
    aside = give_back(d ^ 1).astype(BF16)
    near[: n // 2] = jnp.where(zero, aside[: n // 2], aside[n // 2 :])
    far[:n] = give_back(d ^ jnp.where(zero, ACROSS[0][0], ACROSS[1][0])).astype(BF16)


def far_term(ref, core, n):
    return ref[pl.ds(pl.multiple_of((1 + core) * n, n), n), :]


def pack_back_kernel(far, near, out):
    n = far.shape[0] // 3
    out[:n] = far[:n]
    out[n : 2 * n] = far_term(far, 1 - lax.axis_index("sub"), n)
    out[2 * n :] = near[: n // 2]


def backward_kernel(scale, kept, mine, far, near, there, a, gi, gw, act):
    n = kept.shape[0]
    c = lax.axis_index("sub")
    act[...] = a[...]
    parts = {0: kept[...], 1: jnp.concatenate(in_order(near[: n // 2], there[2 * n :]), axis=0)}
    terms = {0: far_term(mine, c, n), 1: near[n // 2 :]}
    for (dx, _), part, term in zip(
        ACROSS, in_order(far[:n], there[:n]), in_order(far_term(far, c, n), there[n : 2 * n])
    ):
        parts[dx], terms[dx] = part, term

    def total(values):
        values = [values[dx].astype(F32) for dx in range(4)]
        return (values[0] + values[1]) + (values[2] + values[3])

    gw[...] = total(terms) * scale
    gi[...] = total(parts).astype(BF16)


def direct(mesh, adjacency, mask, features, weight, bias, cotangent):
    nodes, feat = features.shape
    sections, width = adjacency.shape[1:]
    total = sections * 2 * width
    half = weight.shape[1]
    x0 = fetch(features, *SHARED[0])
    x1 = fetch(features, *SHARED[1])
    x2 = fetch(features, *SHARED[2])
    give, few, grads, flat = load(adjacency, features, cotangent, mask.transpose(0, 2, 1))
    own = adjacency.transpose(1, 0, 2)
    give = give.transpose(1, 0, 2)
    flat = jnp.pad(flat[:, 0].astype(BF16), ((0, 14), (0, width - sections)))
    give = jnp.concatenate(
        [give.reshape(sections * nodes, width), grads, few, flat],
        axis=0,
    )
    taken = fetch(give, (0, 1))
    xs = [x0, x1, x2]
    q = swap(taken)
    parts = (*xs, weight, grads, bias[None, :])
    (here,) = vmem_call(pack_kernel, [vmem(sum(x.shape[0] for x in parts) + 15, width)], *parts)
    there = swap(here)
    (rows,) = vmem_call(rows_kernel, [vmem(2 * nodes, total)], own, give, taken, q)
    act, far, near, kept = pl.pallas_call(
        forward_kernel,
        out_shape=[
            vmem(nodes, half),
            vmem(3 * nodes, feat),
            vmem(nodes + nodes // 2, feat),
            vmem(nodes, feat, dtype=F32),
        ],
        in_specs=[pl.BlockSpec(memory_space=pltpu.VMEM)] * 6,
        out_specs=[pl.BlockSpec(memory_space=pltpu.VMEM)] * 4,
        scratch_shapes=[vmem(total, feat)],
    )(
        *(
            pltpu.with_memory_space_constraint(x, pltpu.VMEM)
            for x in (rows, features, taken, q, here, there)
        )
    )
    far_, near_ = fetch(far, *ACROSS), fetch(near, (1, 0))
    (packed,) = vmem_call(pack_back_kernel, [vmem(2 * nodes + nodes // 2, feat)], far_, near_)
    packed = swap(packed)
    scale = 1.0 / math.sqrt(total)
    grad_input, grad_weight, activation = pl.pallas_call(
        lambda *refs: backward_kernel(scale, *refs),
        out_shape=[
            jax.ShapeDtypeStruct((nodes, feat), BF16),
            jax.ShapeDtypeStruct((feat, half), F32),
            jax.ShapeDtypeStruct((nodes, half), BF16),
        ],
        in_specs=[pl.BlockSpec(memory_space=pltpu.VMEM)] * 6,
        out_specs=[pl.BlockSpec(memory_space=pltpu.VMEM)] * 3,
    )(
        *(
            pltpu.with_memory_space_constraint(x, pltpu.VMEM)
            for x in (kept, far, far_, near_, packed, act)
        )
    )
    return activation, grad_input, grad_weight


def solution(mesh):
    small = dict(mesh.shape) == {"groups": mesh.shape["groups"], "dom": 4, "rep": 2, "sub": 2}
    body = direct if small else general
    return jax.shard_map(
        lambda *arrays: body(mesh, *arrays),
        mesh=mesh,
        in_specs=(
            P(("groups", "dom"), None, "rep"),
            P(("groups", "dom"), None, "rep"),
            P(("groups", "dom", "rep"), None),
            P(None, "sub"),
            P("sub"),
            P(("groups", "dom", "rep"), "sub"),
        ),
        out_specs=(
            P(("groups", "dom", "rep"), "sub"),
            P(("groups", "dom", "rep"), None),
            P("groups", "sub"),
        ),
        check_vma=False,
    )
```
